32 devices in a mesh: blk: 8 (over z, x), rep: 4 (over y, core).
Axes of the slice: x: 2, y: 2, z: 4, core: 2. Of those that a mesh axis runs over, the one named last changes fastest.
Arguments:
- amplitudes: float32 [64, 64, 16, 512], P('blk', None, 'rep'), may hold values from -6 to 6
- cycle_integrals: float32 [32, 64, 64, 512], P('rep', None, 'blk'), may hold values from -0.046875 to 0.046875
- cross_integrals: float32 [32, 64, 64, 512], P('rep', None, 'blk'), may hold values from -0.046875 to 0.046875
- occ_energy: float32 [64], replicated, may hold values from -2 to -0.5
- vir_energy_a: float32 [32], replicated, may hold values from 0.2 to 3
- vir_energy_b: float32 [16], replicated, may hold values from 0.2 to 3
Outputs:
- update: float32 [64, 32, 16, 64], P('blk', 'rep')
- residual_rms: float32 [], replicated
The draws below stay inside these ranges and needn't reach their ends.
All inputs are finite; a program needn't handle non-finite values.
Results may differ from the reference program's by a relative error of at most 0.0006.
Values sent between devices are 32-bit elements; how exact they have to be, the bound alone decides.
No kernel may reach another device: no remote copies, remote signals or barrier semaphores. Data moves between devices by JAX's collectives and lax.ppermute only.
A program may use at most 128 MiB of HBM per device.

```python
import jax
import jax.numpy as jnp
from jax import lax

O = 64
V = 512
A = 32
B = 16


def raised(drawn, rng, source, target, parts, factor):
    def block_of(axis_at):
        return (jnp.arange(drawn.shape[axis_at]) // (drawn.shape[axis_at] // parts)).reshape((-1,) + (1,) * (drawn.ndim - 1 - axis_at))

    near = jax.random.permutation(rng, parts)[block_of(target)]
    second = (block_of(target) + parts // 2) % parts
    return jnp.where((block_of(source) == near) | (block_of(source) == second), factor * drawn, drawn)


def shard_levels(rng, extent, split, low, largest):
    loudness, own = 1.0, jax.random.fold_in(rng, 6)
    for dim, parts in split:
        heights = jnp.exp(jax.random.uniform(jax.random.fold_in(own, dim), (parts,), jnp.float32, low / len(split), largest / len(split)))
        loudness = loudness * jnp.repeat(heights, extent[dim] // parts).reshape([-1 if axis == dim else 1 for axis in range(len(extent))])
    return loudness


def gaussian(own_key, extent, width, limit, cuts=(), dtype=jnp.bfloat16):
    array = jax.random.normal(own_key, extent, jnp.float32) * width
    if len(cuts) > 0:
        array = shard_levels(own_key, extent, cuts, -0.22, 0.18) * array
    return jnp.clip(array, min=-limit, max=limit).astype(dtype)


def bell_draw_with(key, dims, spread, reach, cuts, heavy, kind=jnp.bfloat16):
    array = spread * jax.random.normal(key, dims, jnp.float32)
    if cuts:
        array = array * shard_levels(key, dims, cuts, -0.22, 0.18)
    return jnp.clip(raised(array, jax.random.fold_in(key, 3), *heavy), -reach, reach).astype(kind)


def setup_inputs(seed: int = 0) -> dict:
    key_of = jax.random.split(jax.random.key(seed), 7)
    amplitudes = gaussian(key_of[0], (O, O, B, V), 1.0, 6.0, ((0, 8), (2, 4)), jnp.float32)
    cycle_integrals = bell_draw_with(key_of[1], (A, O, O, V), (O * V) ** -0.5, 0.046875, ((0, 4), (2, 8)), (2, 1, 8, 2.0), jnp.float32)
    cross_integrals = bell_draw_with(key_of[2], (A, O, O, V), (O * V) ** -0.5, 0.046875, ((0, 4), (2, 8)), (2, 1, 8, 2.0), jnp.float32)
    occ_energy = jnp.clip(jax.random.uniform(key_of[3], (O,), jnp.float32, -2.0, -0.5), -2.0, -0.5)
    vir_energy_a = jnp.clip(jax.random.uniform(key_of[4], (A,), jnp.float32, 0.2, 3.0), 0.2, 3.0)
    vir_energy_b = jnp.clip(jax.random.uniform(key_of[5], (B,), jnp.float32, 0.2, 3.0), 0.2, 3.0)
    return dict(amplitudes=amplitudes, cycle_integrals=cycle_integrals, cross_integrals=cross_integrals, occ_energy=occ_energy, vir_energy_a=vir_energy_a, vir_energy_b=vir_energy_b)


def reference(amplitudes, cycle_integrals, cross_integrals, occ_energy, vir_energy_a, vir_energy_b):
    highest = lax.Precision.HIGHEST
    cycle = jnp.einsum('aikc,kjbc->iabj', cycle_integrals, amplitudes, precision=highest)
    cross = jnp.einsum('aikc,jkbc->iabj', cross_integrals, amplitudes, precision=highest)
    residual = cycle + cross
    denom = occ_energy[:, None, None, None] + occ_energy[None, None, None, :] - vir_energy_a[None, :, None, None] - vir_energy_b[None, None, :, None]
    update = residual / denom
    residual_rms = jnp.sqrt(jnp.sum(residual * residual) / (O * A * B * O))
    return (update, residual_rms)
```

```python
import functools

import jax
import jax.numpy as jnp
from jax import lax
from jax.experimental import pallas as pl
from jax.experimental.pallas import tpu as pltpu
from jax.sharding import PartitionSpec as P

VMEM = 48 * 2**20


def split(x):
    high = x.astype(jnp.bfloat16)
    return high, (x - high.astype(jnp.float32)).astype(jnp.bfloat16)


def split_kernel(in_ref, high_ref, low_ref):
    high_ref[...], low_ref[...] = split(jnp.swapaxes(in_ref[...], 0, 1))


def split_integrals(integrals):
    a, i, k, c = integrals.shape
    tile = 64
    half = jax.ShapeDtypeStruct((k, a * i, c), jnp.bfloat16)
    return pl.pallas_call(
        split_kernel,
        grid=(a * i // tile,),
        in_specs=[pl.BlockSpec((tile, k, c), lambda n: (n, 0, 0))],
        out_specs=[pl.BlockSpec((k, tile, c), lambda n: (0, n, 0))] * 2,
        out_shape=[half, half],
        compiler_params=pltpu.CompilerParams(vmem_limit_bytes=VMEM),
        cost_estimate=pl.CostEstimate(
            flops=4 * integrals.size, bytes_accessed=8 * integrals.size, transcendentals=0
        ),
    )(integrals.reshape(a * i, k, c))


def take_kernel(groups, count, where_ref, in_ref, *out_refs):
    for n in range(count):

        @pl.when(pl.program_id(0) == n)
        def _(n=n):
            for group, out_ref in zip(groups, out_refs):
                if n in group:
                    out_ref[0] = in_ref[:, 0]


def take_blocks(array, where, groups):
    k, q, j, b, c = array.shape
    count = where.shape[0]

    def at(group):
        first, last = group[0], group[-1]
        return lambda n, where: (jnp.clip(n, first, last) - first, 0, 0, 0, 0)

    return pl.pallas_call(
        functools.partial(take_kernel, groups, count),
        grid_spec=pltpu.PrefetchScalarGridSpec(
            num_scalar_prefetch=1,
            grid=(count,),
            in_specs=[pl.BlockSpec((k, 1, j, b, c), lambda n, where: (0, where[n], 0, 0, 0))],
            out_specs=[pl.BlockSpec((1, k, j, b, c), at(group)) for group in groups],
        ),
        out_shape=[
            jax.ShapeDtypeStruct((len(group), k, j, b, c), array.dtype) for group in groups
        ],
        compiler_params=pltpu.CompilerParams(vmem_limit_bytes=VMEM),
        cost_estimate=pl.CostEstimate(
            flops=0, bytes_accessed=12 * count * k * j * b * c, transcendentals=0
        ),
    )(where, array)


def product_kernel(places, first, p_ref, high_ref, low_ref, *refs):
    n = len(places)
    out_ref, t_high, t_low = refs[-3:]
    for ref, (crossed, e, width, ds) in zip(refs, places):
        for at, d in enumerate(ds):
            x = ref[at, :, 0] if crossed else ref[at, 0]
            rows = x.shape[0] * x.shape[1]
            high, low = split(x.reshape(rows, x.shape[2]))
            start = e * width
            if d is not None:
                start = pl.multiple_of(start + (p_ref[0] ^ d) * rows, 32)
            t_high[pl.ds(start, rows), :] = high
            t_low[pl.ds(start, rows), :] = low

    @pl.when(pl.program_id(0) == 0)
    def _():
        out_ref[...] = jnp.zeros_like(out_ref) if first else refs[n][...]

    dot = functools.partial(
        lax.dot_general,
        dimension_numbers=(((1,), (1,)), ((), ())),
        preferred_element_type=jnp.float32,
    )
    out_ref[...] += (
        dot(high_ref[0], t_high[...])
        + dot(high_ref[0], t_low[...])
        + dot(low_ref[0], t_high[...])
    )


def product(halves, sources, start, p, width, columns):
    high, low = halves
    steps, m, c = high.shape
    specs = [pl.BlockSpec((1, m, c), lambda k, p: (k, 0, 0))] * 2
    operands = [high, low]
    places = []
    for stack, crossed, e, ds in sources:
        s = stack.shape
        n = len(ds)
        if crossed:
            specs.append(pl.BlockSpec((n, s[1], 1, s[3], c), lambda k, p: (0, 0, k, 0, 0)))
        else:
            specs.append(pl.BlockSpec((n, 1, s[2], s[3], c), lambda k, p: (0, k, 0, 0, 0)))
        operands.append(stack)
        places.append((crossed, e, width, ds))
    whole = pl.BlockSpec((m, columns), lambda k, p: (0, 0))
    if start is not None:
        specs.append(whole)
        operands.append(start)
    return pl.pallas_call(
        functools.partial(product_kernel, places, start is None),
        grid_spec=pltpu.PrefetchScalarGridSpec(
            num_scalar_prefetch=1,
            grid=(steps,),
            in_specs=specs,
            out_specs=whole,
            scratch_shapes=[pltpu.VMEM((columns, c), jnp.bfloat16)] * 2,
        ),
        out_shape=jax.ShapeDtypeStruct((m, columns), jnp.float32),
        compiler_params=pltpu.CompilerParams(vmem_limit_bytes=VMEM),
        cost_estimate=pl.CostEstimate(
            flops=6 * steps * m * c * columns,
            bytes_accessed=4 * steps * c * (m + columns) + 8 * m * columns,
            transcendentals=0,
        ),
    )(p, *operands)


def shift(value, axis, d):
    size = lax.axis_size(axis)
    return lax.ppermute(value, axis, [(i, i ^ d) for i in range(size)])


def after(value, *others):
    return lax.optimization_barrier((value,) + others)[0]


def scatter_sum(part, bits):
    size, p = lax.axis_size("blk"), lax.axis_index("blk")
    a, i, n = part.shape
    top = size.bit_length() - 1
    part = part.reshape((a,) + (2,) * top + (i // size, n))
    left = list(range(top - 1, -1, -1))
    for bit in bits:
        axis = 1 + left.index(bit)
        mine = (p >> bit) & 1
        away = lax.dynamic_index_in_dim(part, 1 - mine, axis, keepdims=False)
        keep = lax.dynamic_index_in_dim(part, mine, axis, keepdims=False)
        part = keep + shift(away, "blk", 1 << bit)
        left.remove(bit)
    return part


def all_sum(value):
    value = value.reshape(1, 1)
    for axis in ("rep", "blk"):
        d = 1
        while d < lax.axis_size(axis):
            value = value + shift(value, axis, d)
            d *= 2
    return value[0, 0]


def parts_small(amplitudes, cyc, crs, p1, m, width):
    nb = lax.axis_size("blk")
    rows = amplitudes.shape[0]
    mine = amplitudes.reshape((rows, nb, rows) + amplitudes.shape[2:])
    own_a, own_x, t2, t4 = take_blocks(
        mine, p1 ^ jnp.array([1, 3, 2, 4], jnp.int32), [(0, 1, 2, 3), (0, 1), (2,), (3,)]
    )
    own_b, t5, t6, t7 = take_blocks(
        mine, p1 ^ jnp.array([5, 6, 7, 0], jnp.int32), [(0, 1, 2, 3), (0,), (1,), (2,)]
    )
    y_a = shift(own_a, "rep", 2)
    c5 = shift(t5, "blk", 5)
    c6 = shift(t6, "blk", 6)
    row1 = shift(amplitudes[None], "rep", 1)
    u = shift(own_x, "blk", 1)
    c7 = shift(after(t7, c5), "blk", 7)
    y_b = shift(after(own_b, row1), "rep", 2)
    v = shift(jnp.concatenate([t2, u[1:]]), "blk", 2)
    c4 = shift(after(t4, c6), "blk", 4)
    late0 = jnp.concatenate([c5, c6, c7])
    late2 = shift(late0, "rep", 2)
    zu = shift(after(y_a[:2], v), "blk", 1)
    zv = shift(jnp.concatenate([y_a[2:3], zu[1:]]), "blk", 2)
    z4 = shift(after(y_a[3:4], c4), "blk", 4)
    early2 = jnp.concatenate([zu[:1], zv, z4])
    col0 = jnp.concatenate([own_b[3:], u[:1], v, c4, late0])
    col1 = shift(col0, "rep", 1)
    row3a = shift(y_a, "rep", 1)
    row3b = shift(y_b, "rep", 1)
    early3 = shift(early2, "rep", 1)
    late3 = shift(late2, "rep", 1)

    columns = 2 * width
    natural = (None,)
    part0 = product(
        cyc,
        [(amplitudes[None], False, 0, natural), (row1, False, 1, natural)],
        None,
        p1,
        width,
        columns,
    )
    order = (0, 1, 2, 3, 4, 5, 6, 7)
    part0 = product(
        crs, [(col0, True, 0, order), (col1, True, 1, order)], part0, p1, width, columns
    )
    first, second, early, late = (1, 3, 2, 4), (5, 6, 7, 0), (1, 2, 3, 4), (5, 6, 7)
    part1 = product(
        cyc,
        [
            (y_a, False, 0, first),
            (y_b, False, 0, second),
            (row3a, False, 1, first),
            (row3b, False, 1, second),
        ],
        None,
        p1,
        width,
        columns,
    )
    part1 = product(
        crs,
        [
            (y_b[3:], True, 0, (0,)),
            (early2, True, 0, early),
            (late2, True, 0, late),
            (row3b[3:], True, 1, (0,)),
            (early3, True, 1, early),
            (late3, True, 1, late),
        ],
        part1,
        p1,
        width,
        columns,
    )
    return [((0, 1), part0), ((2, 3), part1)]


def parts_large(amplitudes, cyc, crs, p1, m, width):
    nr = lax.axis_size("rep")
    column = lax.all_to_all(amplitudes, "blk", split_axis=1, concat_axis=0, tiled=True)
    parts = []
    for e in range(nr):
        row, col = amplitudes, column
        if e:
            row, col = shift(row, "rep", e), shift(col, "rep", e)
        part = product(cyc, [(row[None], False, 0, (None,))], None, p1, width, width)
        part = product(crs, [(col[None], True, 0, (None,))], part, p1, width, width)
        parts.append(((e,), part))
    return parts


def per_device(
    amplitudes, cycle_integrals, cross_integrals, occ_energy, vir_energy_a, vir_energy_b
):
    nb, nr = lax.axis_size("blk"), lax.axis_size("rep")
    p, r = lax.axis_index("blk"), lax.axis_index("rep")
    rows, o_count, b_count, _ = amplitudes.shape
    a_count = cycle_integrals.shape[0]
    cyc = split_integrals(cycle_integrals)
    crs = split_integrals(cross_integrals)
    p1 = p.astype(jnp.int32).reshape(1)
    width = o_count * b_count
    make = parts_small if (nb, nr, rows) == (8, 4, 8) else parts_large
    residual = jnp.zeros((rows, a_count, nr * b_count, o_count), jnp.float32)
    top = nb.bit_length() - 1
    for es, part in make(amplitudes, cyc, crs, p1, a_count * o_count, width):
        part = scatter_sum(part.reshape(a_count, o_count, -1), range(top))
        part = part.reshape(a_count, rows, len(es), o_count, b_count)
        for at, e in enumerate(es):
            residual = lax.dynamic_update_slice_in_dim(
                residual,
                jnp.transpose(part[:, :, at], (1, 0, 3, 2)),
                (r ^ e) * b_count,
                2,
            )
    occ_local = lax.dynamic_slice_in_dim(occ_energy, p * rows, rows, 0)
    vir_local = lax.dynamic_slice_in_dim(vir_energy_a, r * a_count, a_count, 0)
    denom = (
        occ_local[:, None, None, None]
        + occ_energy[None, None, None, :]
        - vir_local[None, :, None, None]
        - vir_energy_b[None, None, :, None]
    )
    update = residual / denom
    squares = all_sum(jnp.sum(residual * residual))
    total_count = (
        occ_energy.shape[0] * occ_energy.shape[0] * vir_energy_a.shape[0] * vir_energy_b.shape[0]
    )
    residual_rms = jnp.sqrt(squares / total_count)
    return (update, residual_rms)


def solution(mesh):
    return jax.shard_map(
        per_device,
        mesh=mesh,
        in_specs=(
            P("blk", None, "rep", None),
            P("rep", None, "blk", None),
            P("rep", None, "blk", None),
            P(),
            P(),
            P(),
        ),
        out_specs=(P("blk", "rep", None, None), P()),
        check_vma=False,
    )
```

```python
import functools

import jax
import jax.numpy as jnp
from jax import lax
from jax.experimental import pallas as pl
from jax.experimental.pallas import tpu as pltpu
from jax.sharding import PartitionSpec as P

VMEM = 48 * 2**20
QUICK = pl.CostEstimate(flops=2**10, bytes_accessed=2**10, transcendentals=0)


def split(x):
    high = x.astype(jnp.bfloat16)
    return high, (x - high.astype(jnp.float32)).astype(jnp.bfloat16)


def split_kernel(in_ref, high_ref, low_ref):
    high_ref[...], low_ref[...] = split(jnp.swapaxes(in_ref[...], 0, 1))


def split_integrals(integrals):
    a, i, k, c = integrals.shape
    tile = 64
    half = jax.ShapeDtypeStruct((k, a * i, c), jnp.bfloat16)
    return pl.pallas_call(
        split_kernel,
        grid=(a * i // tile,),
        in_specs=[pl.BlockSpec((tile, k, c), lambda n: (n, 0, 0))],
        out_specs=[pl.BlockSpec((k, tile, c), lambda n: (0, n, 0))] * 2,
        out_shape=[half, half],
        compiler_params=pltpu.CompilerParams(vmem_limit_bytes=VMEM),
        cost_estimate=QUICK,
    )(integrals.reshape(a * i, k, c))


def take_kernel(count, where_ref, in_ref, out_ref, held, in_sem, out_sem):
    reads = [
        pltpu.make_async_copy(in_ref.at[:, where_ref[n]], held.at[n], in_sem.at[n])
        for n in range(count)
    ]
    writes = [
        pltpu.make_async_copy(held.at[n], out_ref.at[n], out_sem.at[n]) for n in range(count)
    ]
    for read in reads:
        read.start()
    for read, write in zip(reads, writes):
        read.wait()
        write.start()
    for write in writes:
        write.wait()


def take_blocks(array, where, count):
    k, q, j, b, c = array.shape
    blocks = jax.ShapeDtypeStruct((count, k, j, b, c), array.dtype)
    return pl.pallas_call(
        functools.partial(take_kernel, count),
        grid_spec=pltpu.PrefetchScalarGridSpec(
            num_scalar_prefetch=1,
            grid=(),
            in_specs=[pl.BlockSpec(memory_space=pl.ANY)],
            out_specs=pl.BlockSpec(memory_space=pl.ANY),
            scratch_shapes=[
                pltpu.VMEM(blocks.shape, array.dtype),
                pltpu.SemaphoreType.DMA((count,)),
                pltpu.SemaphoreType.DMA((count,)),
            ],
        ),
        out_shape=blocks,
        compiler_params=pltpu.CompilerParams(vmem_limit_bytes=VMEM),
        cost_estimate=QUICK,
    )(where, array)


def product_kernel(places, first, p_ref, high_ref, low_ref, *refs):
    n = len(places)
    out_ref, t_high, t_low = refs[-3:]
    for ref, (crossed, base, ds) in zip(refs, places):
        for at, d in enumerate(ds):
            x = ref[at, :, 0] if crossed else ref[at, 0]
            rows = x.shape[0] * x.shape[1]
            high, low = split(x.reshape(rows, x.shape[2]))
            start = base
            if d is not None:
                q = d(p_ref[0]) if callable(d) else p_ref[0] ^ d
                start = pl.multiple_of(base + q * rows, 16)
            t_high[pl.ds(start, rows), :] = high
            t_low[pl.ds(start, rows), :] = low

    @pl.when(pl.program_id(0) == 0)
    def _():
        out_ref[...] = jnp.zeros_like(out_ref) if first else refs[n][...]

    dot = functools.partial(
        lax.dot_general,
        dimension_numbers=(((1,), (1,)), ((), ())),
        preferred_element_type=jnp.float32,
    )
    out_ref[...] += (
        dot(high_ref[0], t_high[...])
        + dot(high_ref[0], t_low[...])
        + dot(low_ref[0], t_high[...])
    )


def product(halves, sources, start, p, columns):
    high, low = halves
    steps, m, c = high.shape
    specs = [pl.BlockSpec((1, m, c), lambda k, p: (k, 0, 0))] * 2
    operands = [high, low]
    places = []
    for stack, crossed, base, ds, part, skip in sources:
        b = stack.shape[3]
        n, h = part or (stack.shape[1 if crossed else 2], 0)
        if crossed:
            specs.append(pl.BlockSpec((len(ds), n, 1, b, c), lambda k, p, h=h, skip=skip: (skip, h, k, 0, 0)))
        else:
            specs.append(pl.BlockSpec((len(ds), 1, n, b, c), lambda k, p, h=h, skip=skip: (skip, k, h, 0, 0)))
        operands.append(stack)
        places.append((crossed, base, ds))
    if start is not None:
        specs.append(pl.BlockSpec((m, columns), lambda k, p: (0, start[1])))
        operands.append(start[0])
    return pl.pallas_call(
        functools.partial(product_kernel, places, start is None),
        grid_spec=pltpu.PrefetchScalarGridSpec(
            num_scalar_prefetch=1,
            grid=(steps,),
            in_specs=specs,
            out_specs=pl.BlockSpec((m, columns), lambda k, p: (0, 0)),
            scratch_shapes=[pltpu.VMEM((columns, c), jnp.bfloat16)] * 2,
        ),
        out_shape=jax.ShapeDtypeStruct((m, columns), jnp.float32),
        compiler_params=pltpu.CompilerParams(vmem_limit_bytes=VMEM),
        cost_estimate=QUICK,
    )(p, *operands)


def shift(value, axis, d):
    size = lax.axis_size(axis)
    return lax.ppermute(value, axis, [(i, i ^ d) for i in range(size)])


def after(value, *others):
    return lax.optimization_barrier((value,) + others)[0]


def scatter_sum(part, bits, holds):
    size, p = lax.axis_size("blk"), lax.axis_index("blk")
    a, i, n = part.shape
    top = size.bit_length() - 1
    part = part.reshape((a,) + (2,) * top + (i // size, n))
    left = list(range(top - 1, -1, -1))
    for at, bit in enumerate(bits):
        for hold in holds[: at + len(holds) - len(bits) + 1]:
            part = after(part, hold)
        axis = 1 + left.index(bit)
        mine = (p >> bit) & 1
        away = lax.dynamic_index_in_dim(part, 1 - mine, axis, keepdims=False)
        keep = lax.dynamic_index_in_dim(part, mine, axis, keepdims=False)
        part = keep + shift(away, "blk", 1 << bit)
        left.remove(bit)
    return part


def all_sum(copies):
    return jnp.sum(lax.all_to_all(copies, ("blk", "rep"), 0, 0, tiled=True)[:, 0, 0])


def parts_small(amplitudes, cycle_integrals, cross_integrals, p1):
    nb = lax.axis_size("blk")
    rows, o_count, b_count = amplitudes.shape[:3]
    mine = amplitudes.reshape((rows, nb, rows) + amplitudes.shape[2:])
    own = take_blocks(mine, jnp.arange(nb, dtype=jnp.int32), nb)
    whole = amplitudes[None]
    columns = 2 * o_count * b_count
    half = columns // 2

    def natural(stack):
        return stack.reshape((1, -1) + stack.shape[2:])

    row2 = shift(whole, "rep", 2)
    row1 = shift(whole, "rep", 1)
    col0 = lax.all_to_all(own, "blk", 0, 0, tiled=True)
    cyc = split_integrals(cycle_integrals)
    part0 = product(
        cyc,
        [(whole, False, 0, (None,), None, 0), (row1, False, half, (None,), None, 0)],
        None,
        p1,
        columns,
    )
    crs = split_integrals(after(cross_integrals, part0))

    col0, row2 = after(col0, crs[0]), after(row2, crs[0])
    late0 = take_blocks(
        col0.reshape((1, nb, rows * rows) + amplitudes.shape[2:]),
        p1 ^ jnp.array([5, 6, 7], jnp.int32),
        3,
    )
    late2 = shift(late0.reshape((3,) + col0.shape[1:]), "rep", 2)
    col1 = shift(col0, "rep", 1)
    row3 = shift(row2, "rep", 1)
    rows_in = after(row2, late0).reshape(mine.shape)
    near0 = take_blocks(rows_in, (p1 & 4) | jnp.arange(4, dtype=jnp.int32), 4)
    far0 = take_blocks(rows_in, p1 ^ 4, 1)
    groups = [[0, 1, 2, 3], [4, 5, 6, 7]]
    near2 = lax.all_to_all(near0, "blk", 0, 0, axis_index_groups=groups, tiled=True)
    far2 = shift(far0, "blk", 4)

    sources = [
        (natural(col0), True, 0, (None,), None, 0),
        (natural(col1), True, half, (None,), None, 0),
    ]
    part0 = product(crs, sources, (part0, 0), p1, columns)
    sources = [(row2, False, 0, (None,), None, 0), (row3, False, half, (None,), None, 0)]
    part1 = product(cyc, sources, None, after(p1, part0), columns)

    near3 = shift(after(near2, part1, late2), "rep", 1)
    far3 = shift(after(far2, part1), "rep", 1)
    late3 = shift(after(late2, far3), "rep", 1)
    places = tuple((lambda p, g=g: (p & 4) | g) for g in range(4))
    sources = []
    for base, near, far, late in ((0, near2, far2, late2), (half, near3, far3, late3)):
        sources.append((near, True, base, places, None, 0))
        sources.append((far, True, base, (4,), None, 0))
        sources.append((late, True, base, (5, 6, 7), None, 0))
    part1 = product(crs, sources, (part1, 0), p1, columns)
    return [((0, 1), part0, (late3, part1)), ((2, 3), part1, ())]


def parts_large(amplitudes, cycle_integrals, cross_integrals, p1):
    column = lax.all_to_all(amplitudes, "blk", split_axis=1, concat_axis=0, tiled=True)
    cyc, crs = split_integrals(cycle_integrals), split_integrals(cross_integrals)
    columns = amplitudes.shape[1] * amplitudes.shape[2]
    parts = []
    for e in range(lax.axis_size("rep")):
        row, col = amplitudes, column
        if e:
            row, col = shift(row, "rep", e), shift(col, "rep", e)
        part = product(cyc, [(row[None], False, 0, (None,), None, 0)], None, p1, columns)
        part = product(crs, [(col[None], True, 0, (None,), None, 0)], (part, 0), p1, columns)
        parts.append(((e,), part, ()))
    return parts


def per_device(
    amplitudes, cycle_integrals, cross_integrals, occ_energy, vir_energy_a, vir_energy_b
):
    nb, nr = lax.axis_size("blk"), lax.axis_size("rep")
    p, r = lax.axis_index("blk"), lax.axis_index("rep")
    rows, o_count, b_count, _ = amplitudes.shape
    a_count = cycle_integrals.shape[0]
    p1 = p.astype(jnp.int32).reshape(1)
    make = parts_small if (nb, nr, rows) == (8, 4, 8) else parts_large
    bits = tuple(range(nb.bit_length() - 1))
    squares = jnp.float32(0)
    residual = jnp.zeros((rows, a_count, nr * b_count, o_count), jnp.float32)
    found = []
    for es, part, holds in make(amplitudes, cycle_integrals, cross_integrals, p1):
        part = part.reshape(a_count, o_count, -1)
        half = part.shape[2] // 2
        part = [
            scatter_sum(part[:, :, :half], bits, holds),
            scatter_sum(part[:, :, half:], bits[1:] + bits[:1], holds),
        ]
        squares += jnp.sum(part[0] * part[0]) + jnp.sum(part[1] * part[1])
        found.append((es, part))
    copies = jnp.broadcast_to(squares, (nb * nr, 8, 128))
    es, part = found[-1]
    found[-1] = es, [after(piece, copies) for piece in part]
    for es, part in found:
        part = jnp.concatenate(part, axis=2)
        part = part.reshape(a_count, rows, len(es), o_count, b_count)
        for at, e in enumerate(es):
            residual = lax.dynamic_update_slice_in_dim(
                residual, jnp.transpose(part[:, :, at], (1, 0, 3, 2)), (r ^ e) * b_count, 2
            )
    occ_local = lax.dynamic_slice_in_dim(occ_energy, p * rows, rows, 0)
    vir_local = lax.dynamic_slice_in_dim(vir_energy_a, r * a_count, a_count, 0)
    denom = (
        occ_local[:, None, None, None]
        + occ_energy[None, None, None, :]
        - vir_local[None, :, None, None]
        - vir_energy_b[None, None, :, None]
    )
    update = residual / denom
    squares = all_sum(copies)
    total_count = (
        occ_energy.shape[0] * occ_energy.shape[0] * vir_energy_a.shape[0] * vir_energy_b.shape[0]
    )
    residual_rms = jnp.sqrt(squares / total_count)
    return (update, residual_rms)


def solution(mesh):
    return jax.shard_map(
        per_device,
        mesh=mesh,
        in_specs=(
            P("blk", None, "rep", None),
            P("rep", None, "blk", None),
            P("rep", None, "blk", None),
            P(),
            P(),
            P(),
        ),
        out_specs=(P("blk", "rep", None, None), P()),
        check_vma=False,
    )
```

```python
import functools

import jax
import jax.numpy as jnp
from jax import lax
from jax.experimental import pallas as pl
from jax.experimental.pallas import tpu as pltpu
from jax.sharding import PartitionSpec as P

VMEM = 48 * 2**20
QUICK = pl.CostEstimate(flops=2**10, bytes_accessed=2**10, transcendentals=0)


def split(x):
    high = x.astype(jnp.bfloat16)
    return high, (x - high.astype(jnp.float32)).astype(jnp.bfloat16)


def split_kernel(in_ref, high_ref, low_ref):
    a = in_ref.shape[0]
    for i in range(in_ref.shape[1]):
        high, low = split(jnp.swapaxes(in_ref[:, i], 0, 1))
        high_ref[:, i * a : (i + 1) * a, :] = high
        low_ref[:, i * a : (i + 1) * a, :] = low


def split_integrals(integrals):
    a, i, k, c = integrals.shape
    tile = 8
    half = jax.ShapeDtypeStruct((k, i * a, c), jnp.bfloat16)
    return pl.pallas_call(
        split_kernel,
        grid=(i // tile,),
        in_specs=[pl.BlockSpec((a, tile, k, c), lambda n: (0, n, 0, 0))],
        out_specs=[pl.BlockSpec((k, tile * a, c), lambda n: (0, n, 0))] * 2,
        out_shape=[half, half],
        compiler_params=pltpu.CompilerParams(vmem_limit_bytes=VMEM),
        cost_estimate=QUICK,
    )(integrals)


def take_kernel(count, where_ref, in_ref, out_ref, held, in_sem, out_sem):
    reads = [
        pltpu.make_async_copy(in_ref.at[:, where_ref[n]], held.at[n], in_sem.at[n])
        for n in range(count)
    ]
    writes = [
        pltpu.make_async_copy(held.at[n], out_ref.at[n], out_sem.at[n]) for n in range(count)
    ]
    for read in reads:
        read.start()
    for read, write in zip(reads, writes):
        read.wait()
        write.start()
    for write in writes:
        write.wait()


def take_blocks(array, where, count):
    k, q, j, b, c = array.shape
    blocks = jax.ShapeDtypeStruct((count, k, j, b, c), array.dtype)
    return pl.pallas_call(
        functools.partial(take_kernel, count),
        grid_spec=pltpu.PrefetchScalarGridSpec(
            num_scalar_prefetch=1,
            grid=(),
            in_specs=[pl.BlockSpec(memory_space=pl.ANY)],
            out_specs=pl.BlockSpec(memory_space=pl.ANY),
            scratch_shapes=[
                pltpu.VMEM(blocks.shape, array.dtype),
                pltpu.SemaphoreType.DMA((count,)),
                pltpu.SemaphoreType.DMA((count,)),
            ],
        ),
        out_shape=blocks,
        compiler_params=pltpu.CompilerParams(vmem_limit_bytes=VMEM),
        cost_estimate=QUICK,
    )(where, array)


def product_kernel(places, first, width, p_ref, high_ref, low_ref, *refs):
    out_ref, *t_all = refs[len(places) + (not first) :]
    for ref, (crossed, base, ds) in zip(refs, places):
        for at, d in enumerate(ds):
            for k, t_ref in enumerate(t_all):
                x = ref[at, :, k] if crossed else ref[at, k]
                j, b, _ = x.shape
                q = 0 if d is None else p_ref[0] ^ d
                for n in range(b):
                    start = pl.multiple_of(base + n * width + q * j, 8)
                    t_ref[pl.ds(start, j), :] = x[:, n, :]

    @pl.when(pl.program_id(0) == 0)
    def _():
        out_ref[...] = jnp.zeros_like(out_ref) if first else refs[len(places)][...]

    dot = functools.partial(
        lax.dot_general,
        dimension_numbers=(((1,), (1,)), ((), ())),
        preferred_element_type=jnp.float32,
    )
    total = 0.0
    for k, t_ref in enumerate(t_all):
        t_high, t_low = split(t_ref[...])
        total += dot(high_ref[k], t_high) + dot(high_ref[k], t_low) + dot(low_ref[k], t_high)
    out_ref[...] += total


def product(halves, sources, start, p, width, columns):
    high, low = halves
    steps, m, c = high.shape
    ks = 2 if steps % 2 == 0 else 1
    specs = [pl.BlockSpec((ks, m, c), lambda k, p: (k, 0, 0))] * 2
    operands = [high, low]
    places = []
    for stack, crossed, base, ds, part, skip in sources:
        b = stack.shape[3]
        n, h = part or (stack.shape[1 if crossed else 2], 0)
        if crossed:
            specs.append(pl.BlockSpec((len(ds), n, ks, b, c), lambda k, p, h=h, skip=skip: (skip, h, k, 0, 0)))
        else:
            specs.append(pl.BlockSpec((len(ds), ks, n, b, c), lambda k, p, h=h, skip=skip: (skip, k, h, 0, 0)))
        operands.append(stack)
        places.append((crossed, base, ds))
    if start is not None:
        specs.append(pl.BlockSpec((m, columns), lambda k, p: (0, start[1])))
        operands.append(start[0])
    return pl.pallas_call(
        functools.partial(product_kernel, places, start is None, width),
        grid_spec=pltpu.PrefetchScalarGridSpec(
            num_scalar_prefetch=1,
            grid=(steps // ks,),
            in_specs=specs,
            out_specs=pl.BlockSpec((m, columns), lambda k, p: (0, 0)),
            scratch_shapes=[pltpu.VMEM((columns, c), jnp.float32)] * ks,
        ),
        out_shape=jax.ShapeDtypeStruct((m, columns), jnp.float32),
        compiler_params=pltpu.CompilerParams(vmem_limit_bytes=VMEM),
        cost_estimate=QUICK,
    )(p, *operands)


def shift(value, axis, d):
    size = lax.axis_size(axis)
    return lax.ppermute(value, axis, [(i, i ^ d) for i in range(size)])


def after(value, *others):
    return lax.optimization_barrier((value,) + others)[0]


def scatter_step(part, left, bit, hold=None):
    mine = (lax.axis_index("blk") >> bit) & 1
    axis = left.index(bit)
    away = lax.dynamic_index_in_dim(part, 1 - mine, axis, keepdims=False)
    keep = lax.dynamic_index_in_dim(part, mine, axis, keepdims=False)
    away = shift(away, "blk", 1 << bit)
    if hold is not None:
        away = after(away, hold)
    return keep + away, [other for other in left if other != bit]


def scatter_halves(part, pieces=2):
    size = lax.axis_size("blk")
    bits = tuple(range(size.bit_length() - 1))
    half = part.shape[1] // pieces
    left = list(reversed(bits))
    return [
        (part[:, at : at + half].reshape((2,) * len(bits) + (-1, half)), left, order)
        for at, order in ((0, bits), (half, bits[1:] + bits[:1]))[:pieces]
    ]


def scatter_rest(halves, holds=()):
    for step in range(len(halves[0][2])):
        hold = holds[step] if step < len(holds) else None
        halves = [
            scatter_step(part, left, order[0], hold) + (order[1:],)
            for part, left, order in halves
        ]
    return [part for part, _, _ in halves]


def all_sum(copies):
    return jnp.sum(lax.all_to_all(copies, ("blk", "rep"), 0, 0, tiled=True))


def parts_small(amplitudes, cycle_integrals, cross_integrals, p1):
    nb = lax.axis_size("blk")
    rows, o_count, b_count = amplitudes.shape[:3]
    mine = amplitudes.reshape((rows, nb, rows) + amplitudes.shape[2:])
    own = take_blocks(mine, jnp.arange(nb, dtype=jnp.int32), nb)
    whole = amplitudes[None]
    columns = 2 * o_count * b_count
    half = columns // 2

    def natural(stack):
        return stack.reshape((1, -1) + stack.shape[2:])

    row2 = shift(whole, "rep", 2)
    row1 = shift(whole, "rep", 1)
    col0 = lax.all_to_all(own, "blk", 0, 0, tiled=True)
    cyc = split_integrals(cycle_integrals)
    part0 = product(
        cyc,
        [(whole, False, 0, (None,), None, 0), (row1, False, half, (None,), None, 0)],
        None,
        p1,
        o_count,
        columns,
    )
    crs = split_integrals(after(cross_integrals, part0))

    row2 = after(row2, crs[0])
    row3 = shift(row2, "rep", 1)
    rows_in = row2.reshape(mine.shape)
    near = [take_blocks(rows_in, p1 ^ d, 1) for d in (0, 1, 2, 3, 4)]
    near[1] = shift(near[1], "blk", 1)
    col0 = after(col0, row3, *near)
    late0 = take_blocks(
        col0.reshape((1, nb, rows * rows) + amplitudes.shape[2:]),
        p1 ^ jnp.array([5, 6, 7], jnp.int32),
        3,
    )
    late2 = shift(late0.reshape((3,) + col0.shape[1:]), "rep", 2)
    col1 = shift(col0, "rep", 1)
    near[2] = shift(after(near[2], late0), "blk", 2)
    near[3] = shift(after(near[3], late0), "blk", 3)
    far2 = shift(after(near[4], late0), "blk", 4)

    sources = [(row2, False, 0, (None,), None, 0), (row3, False, half, (None,), None, 0)]
    part1 = product(cyc, sources, None, after(p1, late0), o_count, columns)
    sources = [
        (natural(col0), True, 0, (None,), None, 0),
        (natural(col1), True, half, (None,), None, 0),
    ]
    part0 = product(crs, sources, (part0, 0), after(p1, part1), o_count, columns)
    sums0 = scatter_halves(part0, 1)
    sums0 = [
        scatter_step(part, left, order[0]) + (order[1:],) for part, left, order in sums0
    ]

    begun = [part for part, _, _ in sums0]
    far3 = shift(after(far2, part0), "rep", 1)
    late3 = shift(after(late2, far3, *begun), "rep", 1)
    early2 = jnp.concatenate(near[:2] + [after(near[2], part0), after(near[3], part0)])
    early3 = shift(early2, "rep", 1)
    sources = []
    for base, early, far, late in ((0, early2, far2, late2), (half, early3, far3, late3)):
        sources.append((early, True, base, (0, 1, 2, 3), None, 0))
        sources.append((far, True, base, (4,), None, 0))
        sources.append((late, True, base, (5, 6, 7), None, 0))
    ready = after(p1, *begun)
    part1 = product(crs, sources, (part1, 0), ready, o_count, columns)
    done = scatter_rest(sums0, (part1,))
    return [((0, 1), done), ((2, 3), scatter_rest(scatter_halves(part1)))]


def parts_large(amplitudes, cycle_integrals, cross_integrals, p1):
    column = lax.all_to_all(amplitudes, "blk", split_axis=1, concat_axis=0, tiled=True)
    cyc, crs = split_integrals(cycle_integrals), split_integrals(cross_integrals)
    o_count = amplitudes.shape[1]
    columns = o_count * amplitudes.shape[2]
    parts = []
    for e in range(lax.axis_size("rep")):
        row, col = amplitudes, column
        if e:
            row, col = shift(row, "rep", e), shift(col, "rep", e)
        part = product(cyc, [(row[None], False, 0, (None,), None, 0)], None, p1, o_count, columns)
        part = product(crs, [(col[None], True, 0, (None,), None, 0)], (part, 0), p1, o_count, columns)
        parts.append(((e,), scatter_rest(scatter_halves(part))))
    return parts


def per_device(
    amplitudes, cycle_integrals, cross_integrals, occ_energy, vir_energy_a, vir_energy_b
):
    nb, nr = lax.axis_size("blk"), lax.axis_size("rep")
    p, r = lax.axis_index("blk"), lax.axis_index("rep")
    rows, o_count, b_count, _ = amplitudes.shape
    a_count = cycle_integrals.shape[0]
    p1 = p.astype(jnp.int32).reshape(1)
    make = parts_small if (nb, nr, rows) == (8, 4, 8) else parts_large
    residual = jnp.zeros((rows, a_count, nr * b_count, o_count), jnp.float32)
    found = make(amplitudes, cycle_integrals, cross_integrals, p1)
    squares = sum(
        jnp.sum((part * part).reshape(-1, o_count), axis=0) for _, parts in found for part in parts
    )
    copies = jnp.broadcast_to(squares, (nb * nr,) + squares.shape)
    es, parts = found[-1]
    found[-1] = es, [after(part, copies) for part in parts]
    for es, parts in found:
        part = jnp.concatenate(parts, axis=1) if len(parts) > 1 else parts[0]
        part = part.reshape(rows, a_count, len(es), b_count, o_count)
        for at, e in enumerate(es):
            residual = lax.dynamic_update_slice_in_dim(
                residual, part[:, :, at], (r ^ e) * b_count, 2
            )
    occ_local = lax.dynamic_slice_in_dim(occ_energy, p * rows, rows, 0)
    vir_local = lax.dynamic_slice_in_dim(vir_energy_a, r * a_count, a_count, 0)
    denom = (
        occ_local[:, None, None, None]
        + occ_energy[None, None, None, :]
        - vir_local[None, :, None, None]
        - vir_energy_b[None, None, :, None]
    )
    update = residual / denom
    squares = all_sum(copies)
    total_count = (
        occ_energy.shape[0] * occ_energy.shape[0] * vir_energy_a.shape[0] * vir_energy_b.shape[0]
    )
    residual_rms = jnp.sqrt(squares / total_count)
    return (update, residual_rms)


def solution(mesh):
    return jax.shard_map(
        per_device,
        mesh=mesh,
        in_specs=(
            P("blk", None, "rep", None),
            P("rep", None, "blk", None),
            P("rep", None, "blk", None),
            P(),
            P(),
            P(),
        ),
        out_specs=(P("blk", "rep", None, None), P()),
        check_vma=False,
    )
```

```python
import functools

import jax
import jax.numpy as jnp
from jax import lax
from jax.experimental import pallas as pl
from jax.experimental.pallas import tpu as pltpu
from jax.sharding import PartitionSpec as P

VMEM = 48 * 2**20
QUICK = pl.CostEstimate(flops=2**10, bytes_accessed=2**10, transcendentals=0)


def split(x):
    high = x.astype(jnp.bfloat16)
    return high, (x - high.astype(jnp.float32)).astype(jnp.bfloat16)


def split_kernel(in_ref, high_ref, low_ref):
    a = in_ref.shape[0]
    for i in range(in_ref.shape[1]):
        high, low = split(jnp.swapaxes(in_ref[:, i], 0, 1))
        high_ref[:, i * a : (i + 1) * a, :] = high
        low_ref[:, i * a : (i + 1) * a, :] = low


def split_integrals(integrals):
    a, i, k, c = integrals.shape
    tile = 8
    half = jax.ShapeDtypeStruct((k, i * a, c), jnp.bfloat16)
    return pl.pallas_call(
        split_kernel,
        grid=(i // tile,),
        in_specs=[pl.BlockSpec((a, tile, k, c), lambda n: (0, n, 0, 0))],
        out_specs=[pl.BlockSpec((k, tile * a, c), lambda n: (0, n, 0))] * 2,
        out_shape=[half, half],
        compiler_params=pltpu.CompilerParams(vmem_limit_bytes=VMEM),
        cost_estimate=QUICK,
    )(integrals)


def take_kernel(count, where_ref, in_ref, out_ref, held, in_sem, out_sem):
    reads = [
        pltpu.make_async_copy(in_ref.at[:, where_ref[n]], held.at[n], in_sem.at[n])
        for n in range(count)
    ]
    writes = [
        pltpu.make_async_copy(held.at[n], out_ref.at[n], out_sem.at[n]) for n in range(count)
    ]
    for read in reads:
        read.start()
    for read, write in zip(reads, writes):
        read.wait()
        write.start()
    for write in writes:
        write.wait()


def take_blocks(array, where, count):
    k, q, j, b, c = array.shape
    blocks = jax.ShapeDtypeStruct((count, k, j, b, c), array.dtype)
    return pl.pallas_call(
        functools.partial(take_kernel, count),
        grid_spec=pltpu.PrefetchScalarGridSpec(
            num_scalar_prefetch=1,
            grid=(),
            in_specs=[pl.BlockSpec(memory_space=pl.ANY)],
            out_specs=pl.BlockSpec(memory_space=pl.ANY),
            scratch_shapes=[
                pltpu.VMEM(blocks.shape, array.dtype),
                pltpu.SemaphoreType.DMA((count,)),
                pltpu.SemaphoreType.DMA((count,)),
            ],
        ),
        out_shape=blocks,
        compiler_params=pltpu.CompilerParams(vmem_limit_bytes=VMEM),
        cost_estimate=QUICK,
    )(where, array)


def product_kernel(places, first, width, p_ref, high_ref, low_ref, *refs):
    out_ref, *t_all = refs[len(places) + (not first) :]
    for ref, (crossed, base, ds) in zip(refs, places):
        for at, d in enumerate(ds):
            for k, t_ref in enumerate(t_all):
                x = ref[at, :, k] if crossed else ref[at, k]
                j, b, _ = x.shape
                q = 0 if d is None else p_ref[0] ^ d
                for n in range(b):
                    start = pl.multiple_of(base + n * width + q * j, 8)
                    t_ref[pl.ds(start, j), :] = x[:, n, :]

    @pl.when(pl.program_id(0) == 0)
    def _():
        out_ref[...] = jnp.zeros_like(out_ref) if first else refs[len(places)][...]

    dot = functools.partial(
        lax.dot_general,
        dimension_numbers=(((1,), (1,)), ((), ())),
        preferred_element_type=jnp.float32,
    )
    total = 0.0
    for k, t_ref in enumerate(t_all):
        t_high, t_low = split(t_ref[...])
        total += dot(high_ref[k], t_high) + dot(high_ref[k], t_low) + dot(low_ref[k], t_high)
    out_ref[...] += total


def product(halves, sources, start, p, width, columns):
    high, low = halves
    steps, m, c = high.shape
    ks = 2 if steps % 2 == 0 else 1
    specs = [pl.BlockSpec((ks, m, c), lambda k, p: (k, 0, 0))] * 2
    operands = [high, low]
    places = []
    for stack, crossed, base, ds, part, skip in sources:
        b = stack.shape[3]
        n, h = part or (stack.shape[1 if crossed else 2], 0)
        if crossed:
            specs.append(pl.BlockSpec((len(ds), n, ks, b, c), lambda k, p, h=h, skip=skip: (skip, h, k, 0, 0)))
        else:
            specs.append(pl.BlockSpec((len(ds), ks, n, b, c), lambda k, p, h=h, skip=skip: (skip, k, h, 0, 0)))
        operands.append(stack)
        places.append((crossed, base, ds))
    if start is not None:
        specs.append(pl.BlockSpec((m, columns), lambda k, p: (0, start[1])))
        operands.append(start[0])
    return pl.pallas_call(
        functools.partial(product_kernel, places, start is None, width),
        grid_spec=pltpu.PrefetchScalarGridSpec(
            num_scalar_prefetch=1,
            grid=(steps // ks,),
            in_specs=specs,
            out_specs=pl.BlockSpec((m, columns), lambda k, p: (0, 0)),
            scratch_shapes=[pltpu.VMEM((columns, c), jnp.float32)] * ks,
        ),
        out_shape=jax.ShapeDtypeStruct((m, columns), jnp.float32),
        compiler_params=pltpu.CompilerParams(vmem_limit_bytes=VMEM),
        cost_estimate=QUICK,
    )(p, *operands)


def shift(value, axis, d):
    size = lax.axis_size(axis)
    return lax.ppermute(value, axis, [(i, i ^ d) for i in range(size)])


def after(value, *others):
    return lax.optimization_barrier((value,) + others)[0]


def scatter_step(part, left, bit, hold=None):
    mine = (lax.axis_index("blk") >> bit) & 1
    axis = left.index(bit)
    away = lax.dynamic_index_in_dim(part, 1 - mine, axis, keepdims=False)
    keep = lax.dynamic_index_in_dim(part, mine, axis, keepdims=False)
    away = shift(away, "blk", 1 << bit)
    if hold is not None:
        away = after(away, hold)
    return keep + away, [other for other in left if other != bit]


def scatter_halves(part, pieces=2):
    size = lax.axis_size("blk")
    bits = tuple(range(size.bit_length() - 1))
    half = part.shape[1] // pieces
    left = list(reversed(bits))
    return [
        (part[:, at : at + half].reshape((2,) * len(bits) + (-1, half)), left, order)
        for at, order in ((0, bits), (half, bits[1:] + bits[:1]))[:pieces]
    ]


def scatter_rest(halves, holds=()):
    for step in range(len(halves[0][2])):
        hold = holds[step] if step < len(holds) else None
        halves = [
            scatter_step(part, left, order[0], hold) + (order[1:],)
            for part, left, order in halves
        ]
    return [part for part, _, _ in halves]


def all_sum(copies):
    return jnp.sum(lax.all_to_all(copies, ("blk", "rep"), 0, 0, tiled=True))


def parts_small(amplitudes, cycle_integrals, cross_integrals, p1):
    nb = lax.axis_size("blk")
    rows, o_count, b_count = amplitudes.shape[:3]
    mine = amplitudes.reshape((rows, nb, rows) + amplitudes.shape[2:])
    own = take_blocks(mine, jnp.arange(nb, dtype=jnp.int32), nb)
    whole = amplitudes[None]
    columns = 2 * o_count * b_count
    half = columns // 2

    def natural(stack):
        return stack.reshape((1, -1) + stack.shape[2:])

    row2 = shift(whole, "rep", 2)
    row1 = shift(whole, "rep", 1)
    col0 = lax.all_to_all(own, "blk", 0, 0, tiled=True)
    cyc = split_integrals(cycle_integrals)
    part0 = product(
        cyc,
        [(whole, False, 0, (None,), None, 0), (row1, False, half, (None,), None, 0)],
        None,
        p1,
        o_count,
        columns,
    )
    crs = split_integrals(after(cross_integrals, part0))

    row2 = after(row2, crs[0])
    row3 = shift(row2, "rep", 1)
    rows_in = row2.reshape(mine.shape)
    near = [take_blocks(rows_in, p1 ^ d, 1) for d in (0, 1, 2, 3, 4)]
    col0 = after(col0, row3, *near)
    late0 = take_blocks(
        col0.reshape((1, nb, rows * rows) + amplitudes.shape[2:]),
        p1 ^ jnp.array([5, 6, 7], jnp.int32),
        3,
    )
    late2 = shift(late0.reshape((3,) + col0.shape[1:]), "rep", 2)
    col1 = shift(col0, "rep", 1)
    near[1] = shift(after(near[1], col1), "blk", 1)
    near[2] = shift(after(near[2], late0), "blk", 2)
    near[3] = shift(after(near[3], late0), "blk", 3)
    far2 = shift(after(near[4], late0), "blk", 4)

    sources = [(row2, False, 0, (None,), None, 0), (row3, False, half, (None,), None, 0)]
    part1 = product(cyc, sources, None, after(p1, late0), o_count, columns)
    sources = [
        (natural(col0), True, 0, (None,), None, 0),
        (natural(col1), True, half, (None,), None, 0),
    ]
    part0 = product(crs, sources, (part0, 0), after(p1, part1), o_count, columns)
    sums0 = scatter_halves(part0, 1)
    sums0 = [
        scatter_step(part, left, order[0]) + (order[1:],) for part, left, order in sums0
    ]

    begun = [part for part, _, _ in sums0]
    far3 = shift(after(far2, part0), "rep", 1)
    late3 = shift(after(late2, far3, *begun), "rep", 1)
    early2 = jnp.concatenate(near[:1] + [after(part, part0) for part in near[1:4]])
    early3 = shift(early2, "rep", 1)
    sources = []
    for base, early, far, late in ((0, early2, far2, late2), (half, early3, far3, late3)):
        sources.append((early, True, base, (0, 1, 2, 3), None, 0))
        sources.append((far, True, base, (4,), None, 0))
        sources.append((late, True, base, (5, 6, 7), None, 0))
    ready = after(p1, *begun)
    part1 = product(crs, sources, (part1, 0), ready, o_count, columns)
    done = scatter_rest(sums0, (part1,))
    return [((0, 1), done), ((2, 3), scatter_rest(scatter_halves(part1)))]


def parts_large(amplitudes, cycle_integrals, cross_integrals, p1):
    column = lax.all_to_all(amplitudes, "blk", split_axis=1, concat_axis=0, tiled=True)
    cyc, crs = split_integrals(cycle_integrals), split_integrals(cross_integrals)
    o_count = amplitudes.shape[1]
    columns = o_count * amplitudes.shape[2]
    parts = []
    for e in range(lax.axis_size("rep")):
        row, col = amplitudes, column
        if e:
            row, col = shift(row, "rep", e), shift(col, "rep", e)
        part = product(cyc, [(row[None], False, 0, (None,), None, 0)], None, p1, o_count, columns)
        part = product(crs, [(col[None], True, 0, (None,), None, 0)], (part, 0), p1, o_count, columns)
        parts.append(((e,), scatter_rest(scatter_halves(part))))
    return parts


def per_device(
    amplitudes, cycle_integrals, cross_integrals, occ_energy, vir_energy_a, vir_energy_b
):
    nb, nr = lax.axis_size("blk"), lax.axis_size("rep")
    p, r = lax.axis_index("blk"), lax.axis_index("rep")
    rows, o_count, b_count, _ = amplitudes.shape
    a_count = cycle_integrals.shape[0]
    p1 = p.astype(jnp.int32).reshape(1)
    make = parts_small if (nb, nr, rows) == (8, 4, 8) else parts_large
    residual = jnp.zeros((rows, a_count, nr * b_count, o_count), jnp.float32)
    found = make(amplitudes, cycle_integrals, cross_integrals, p1)
    squares = sum(
        jnp.sum((part * part).reshape(-1, o_count), axis=0) for _, parts in found for part in parts
    )
    copies = jnp.broadcast_to(squares, (nb * nr,) + squares.shape)
    es, parts = found[-1]
    found[-1] = es, [after(part, copies) for part in parts]
    for es, parts in found:
        part = jnp.concatenate(parts, axis=1) if len(parts) > 1 else parts[0]
        part = part.reshape(rows, a_count, len(es), b_count, o_count)
        for at, e in enumerate(es):
            residual = lax.dynamic_update_slice_in_dim(
                residual, part[:, :, at], (r ^ e) * b_count, 2
            )
    occ_local = lax.dynamic_slice_in_dim(occ_energy, p * rows, rows, 0)
    vir_local = lax.dynamic_slice_in_dim(vir_energy_a, r * a_count, a_count, 0)
    denom = (
        occ_local[:, None, None, None]
        + occ_energy[None, None, None, :]
        - vir_local[None, :, None, None]
        - vir_energy_b[None, None, :, None]
    )
    update = residual / denom
    squares = all_sum(copies)
    total_count = (
        occ_energy.shape[0] * occ_energy.shape[0] * vir_energy_a.shape[0] * vir_energy_b.shape[0]
    )
    residual_rms = jnp.sqrt(squares / total_count)
    return (update, residual_rms)


def solution(mesh):
    return jax.shard_map(
        per_device,
        mesh=mesh,
        in_specs=(
            P("blk", None, "rep", None),
            P("rep", None, "blk", None),
            P("rep", None, "blk", None),
            P(),
            P(),
            P(),
        ),
        out_specs=(P("blk", "rep", None, None), P()),
        check_vma=False,
    )
```

```python
import functools

import jax
import jax.numpy as jnp
from jax import lax
from jax.experimental import pallas as pl
from jax.experimental.pallas import tpu as pltpu
from jax.sharding import PartitionSpec as P

VMEM = 48 * 2**20
QUICK = pl.CostEstimate(flops=2**10, bytes_accessed=2**10, transcendentals=0)


def split(x):
    high = x.astype(jnp.bfloat16)
    return high, (x - high.astype(jnp.float32)).astype(jnp.bfloat16)


def split_kernel(in_ref, high_ref, low_ref):
    a = in_ref.shape[0]
    for i in range(in_ref.shape[1]):
        high, low = split(jnp.swapaxes(in_ref[:, i], 0, 1))
        high_ref[:, i * a : (i + 1) * a, :] = high
        low_ref[:, i * a : (i + 1) * a, :] = low


def split_integrals(integrals):
    a, i, k, c = integrals.shape
    tile = 8
    half = jax.ShapeDtypeStruct((k, i * a, c), jnp.bfloat16)
    return pl.pallas_call(
        split_kernel,
        grid=(i // tile,),
        in_specs=[pl.BlockSpec((a, tile, k, c), lambda n: (0, n, 0, 0))],
        out_specs=[pl.BlockSpec((k, tile * a, c), lambda n: (0, n, 0))] * 2,
        out_shape=[half, half],
        compiler_params=pltpu.CompilerParams(vmem_limit_bytes=VMEM),
        cost_estimate=QUICK,
    )(integrals)


def take_kernel(count, where_ref, in_ref, out_ref, held, in_sem, out_sem):
    reads = [
        pltpu.make_async_copy(in_ref.at[:, where_ref[n]], held.at[n], in_sem.at[n])
        for n in range(count)
    ]
    writes = [
        pltpu.make_async_copy(held.at[n], out_ref.at[n], out_sem.at[n]) for n in range(count)
    ]
    for read in reads:
        read.start()
    for read, write in zip(reads, writes):
        read.wait()
        write.start()
    for write in writes:
        write.wait()


def take_blocks(array, where, count):
    k, q, j, b, c = array.shape
    blocks = jax.ShapeDtypeStruct((count, k, j, b, c), array.dtype)
    return pl.pallas_call(
        functools.partial(take_kernel, count),
        grid_spec=pltpu.PrefetchScalarGridSpec(
            num_scalar_prefetch=1,
            grid=(),
            in_specs=[pl.BlockSpec(memory_space=pl.ANY)],
            out_specs=pl.BlockSpec(memory_space=pl.ANY),
            scratch_shapes=[
                pltpu.VMEM(blocks.shape, array.dtype),
                pltpu.SemaphoreType.DMA((count,)),
                pltpu.SemaphoreType.DMA((count,)),
            ],
        ),
        out_shape=blocks,
        compiler_params=pltpu.CompilerParams(vmem_limit_bytes=VMEM),
        cost_estimate=QUICK,
    )(where, array)


def product_kernel(places, first, width, p_ref, high_ref, low_ref, *refs):
    out_ref, *t_all = refs[len(places) + (not first) :]
    for ref, (crossed, base, ds) in zip(refs, places):
        for at, d in enumerate(ds):
            for k, t_ref in enumerate(t_all):
                x = ref[at, :, k] if crossed else ref[at, k]
                j, b, _ = x.shape
                q = 0 if d is None else p_ref[0] ^ d
                for n in range(b):
                    start = pl.multiple_of(base + n * width + q * j, 8)
                    t_ref[pl.ds(start, j), :] = x[:, n, :]

    @pl.when(pl.program_id(0) == 0)
    def _():
        out_ref[...] = jnp.zeros_like(out_ref) if first else refs[len(places)][...]

    dot = functools.partial(
        lax.dot_general,
        dimension_numbers=(((1,), (1,)), ((), ())),
        preferred_element_type=jnp.float32,
    )
    total = 0.0
    for k, t_ref in enumerate(t_all):
        t_high, t_low = split(t_ref[...])
        total += dot(high_ref[k], t_high) + dot(high_ref[k], t_low) + dot(low_ref[k], t_high)
    out_ref[...] += total


def product(halves, sources, start, p, width, columns):
    high, low = halves
    steps, m, c = high.shape
    ks = 2 if steps % 2 == 0 else 1
    specs = [pl.BlockSpec((ks, m, c), lambda k, p: (k, 0, 0))] * 2
    operands = [high, low]
    places = []
    for stack, crossed, base, ds, part, skip in sources:
        b = stack.shape[3]
        n, h = part or (stack.shape[1 if crossed else 2], 0)
        if crossed:
            specs.append(pl.BlockSpec((len(ds), n, ks, b, c), lambda k, p, h=h, skip=skip: (skip, h, k, 0, 0)))
        else:
            specs.append(pl.BlockSpec((len(ds), ks, n, b, c), lambda k, p, h=h, skip=skip: (skip, k, h, 0, 0)))
        operands.append(stack)
        places.append((crossed, base, ds))
    if start is not None:
        specs.append(pl.BlockSpec((m, columns), lambda k, p: (0, start[1])))
        operands.append(start[0])
    return pl.pallas_call(
        functools.partial(product_kernel, places, start is None, width),
        grid_spec=pltpu.PrefetchScalarGridSpec(
            num_scalar_prefetch=1,
            grid=(steps // ks,),
            in_specs=specs,
            out_specs=pl.BlockSpec((m, columns), lambda k, p: (0, 0)),
            scratch_shapes=[pltpu.VMEM((columns, c), jnp.float32)] * ks,
        ),
        out_shape=jax.ShapeDtypeStruct((m, columns), jnp.float32),
        compiler_params=pltpu.CompilerParams(vmem_limit_bytes=VMEM),
        cost_estimate=QUICK,
    )(p, *operands)


def shift(value, axis, d):
    size = lax.axis_size(axis)
    return lax.ppermute(value, axis, [(i, i ^ d) for i in range(size)])


def after(value, *others):
    return lax.optimization_barrier((value,) + others)[0]


def scatter_step(part, left, bit, hold=None):
    mine = (lax.axis_index("blk") >> bit) & 1
    axis = left.index(bit)
    away = lax.dynamic_index_in_dim(part, 1 - mine, axis, keepdims=False)
    keep = lax.dynamic_index_in_dim(part, mine, axis, keepdims=False)
    away = shift(away, "blk", 1 << bit)
    if hold is not None:
        away = after(away, hold)
    return keep + away, [other for other in left if other != bit]


def scatter_halves(part, pieces=2):
    size = lax.axis_size("blk")
    bits = tuple(range(size.bit_length() - 1))
    half = part.shape[1] // pieces
    left = list(reversed(bits))
    return [
        (part[:, at : at + half].reshape((2,) * len(bits) + (-1, half)), left, order)
        for at, order in ((0, bits), (half, bits[1:2] + bits[:1] + bits[2:]))[:pieces]
    ]


def scatter_rest(halves, holds=()):
    for step in range(len(halves[0][2])):
        hold = holds[step] if step < len(holds) else None
        halves = [
            scatter_step(part, left, order[0], hold) + (order[1:],)
            for part, left, order in halves
        ]
    return [part for part, _, _ in halves]


def all_sum(copies):
    return jnp.sum(lax.all_to_all(copies, ("blk", "rep"), 0, 0, tiled=True))


def parts_small(amplitudes, cycle_integrals, cross_integrals, p1):
    nb = lax.axis_size("blk")
    rows, o_count, b_count = amplitudes.shape[:3]
    mine = amplitudes.reshape((rows, nb, rows) + amplitudes.shape[2:])
    own = take_blocks(mine, jnp.arange(nb, dtype=jnp.int32), nb)
    whole = amplitudes[None]
    columns = 2 * o_count * b_count
    half = columns // 2

    def natural(stack):
        return stack.reshape((1, -1) + stack.shape[2:])

    row2 = shift(whole, "rep", 2)
    row1 = shift(whole, "rep", 1)
    col0 = lax.all_to_all(own, "blk", 0, 0, tiled=True)
    cyc = split_integrals(cycle_integrals)
    part0 = product(
        cyc,
        [(whole, False, 0, (None,), None, 0), (row1, False, half, (None,), None, 0)],
        None,
        p1,
        o_count,
        columns,
    )
    crs = split_integrals(after(cross_integrals, part0))

    row2 = after(row2, crs[0])
    row3 = shift(row2, "rep", 1)
    rows_in = row2.reshape(mine.shape)
    near = [take_blocks(rows_in, p1 ^ d, 1) for d in (0, 1, 2, 3, 4)]
    col0 = after(col0, row3, *near)
    late0 = take_blocks(
        col0.reshape((1, nb, rows * rows) + amplitudes.shape[2:]),
        p1 ^ jnp.array([5, 6, 7], jnp.int32),
        3,
    )
    late2 = shift(late0.reshape((3,) + col0.shape[1:]), "rep", 2)
    col1 = shift(col0, "rep", 1)
    near[1] = shift(after(near[1], col1), "blk", 1)
    near[2] = shift(after(near[2], late0), "blk", 2)
    near[3] = shift(after(near[3], late0), "blk", 3)
    far2 = shift(after(near[4], late0), "blk", 4)

    sources = [(row2, False, 0, (None,), None, 0), (row3, False, half, (None,), None, 0)]
    part1 = product(cyc, sources, None, after(p1, late0), o_count, columns)
    sources = [
        (natural(col0), True, 0, (None,), None, 0),
        (natural(col1), True, half, (None,), None, 0),
    ]
    part0 = product(crs, sources, (part0, 0), after(p1, part1), o_count, columns)
    sums0 = scatter_halves(part0, 1)
    sums0 = [
        scatter_step(part, left, order[0]) + (order[1:],) for part, left, order in sums0
    ]

    begun = [part for part, _, _ in sums0]
    far3 = shift(after(far2, part0), "rep", 1)
    late3 = shift(after(late2, far3, *begun), "rep", 1)
    early2 = jnp.concatenate(near[:1] + [after(part, part0) for part in near[1:4]])
    early3 = shift(early2, "rep", 1)
    sources = []
    for base, early, far, late in ((0, early2, far2, late2), (half, early3, far3, late3)):
        sources.append((early, True, base, (0, 1, 2, 3), None, 0))
        sources.append((far, True, base, (4,), None, 0))
        sources.append((late, True, base, (5, 6, 7), None, 0))
    ready = after(p1, *begun)
    part1 = product(crs, sources, (part1, 0), ready, o_count, columns)
    done = scatter_rest(sums0, (part1,))
    return [((0, 1), done), ((2, 3), scatter_rest(scatter_halves(part1)))]


def parts_large(amplitudes, cycle_integrals, cross_integrals, p1):
    column = lax.all_to_all(amplitudes, "blk", split_axis=1, concat_axis=0, tiled=True)
    cyc, crs = split_integrals(cycle_integrals), split_integrals(cross_integrals)
    o_count = amplitudes.shape[1]
    columns = o_count * amplitudes.shape[2]
    parts = []
    for e in range(lax.axis_size("rep")):
        row, col = amplitudes, column
        if e:
            row, col = shift(row, "rep", e), shift(col, "rep", e)
        part = product(cyc, [(row[None], False, 0, (None,), None, 0)], None, p1, o_count, columns)
        part = product(crs, [(col[None], True, 0, (None,), None, 0)], (part, 0), p1, o_count, columns)
        parts.append(((e,), scatter_rest(scatter_halves(part))))
    return parts


def per_device(
    amplitudes, cycle_integrals, cross_integrals, occ_energy, vir_energy_a, vir_energy_b
):
    nb, nr = lax.axis_size("blk"), lax.axis_size("rep")
    p, r = lax.axis_index("blk"), lax.axis_index("rep")
    rows, o_count, b_count, _ = amplitudes.shape
    a_count = cycle_integrals.shape[0]
    p1 = p.astype(jnp.int32).reshape(1)
    make = parts_small if (nb, nr, rows) == (8, 4, 8) else parts_large
    residual = jnp.zeros((rows, a_count, nr * b_count, o_count), jnp.float32)
    found = make(amplitudes, cycle_integrals, cross_integrals, p1)
    squares = sum(
        jnp.sum((part * part).reshape(-1, o_count), axis=0) for _, parts in found for part in parts
    )
    copies = jnp.broadcast_to(squares, (nb * nr,) + squares.shape)
    es, parts = found[-1]
    found[-1] = es, [after(part, copies) for part in parts]
    for es, parts in found:
        part = jnp.concatenate(parts, axis=1) if len(parts) > 1 else parts[0]
        part = part.reshape(rows, a_count, len(es), b_count, o_count)
        for at, e in enumerate(es):
            residual = lax.dynamic_update_slice_in_dim(
                residual, part[:, :, at], (r ^ e) * b_count, 2
            )
    occ_local = lax.dynamic_slice_in_dim(occ_energy, p * rows, rows, 0)
    vir_local = lax.dynamic_slice_in_dim(vir_energy_a, r * a_count, a_count, 0)
    denom = (
        occ_local[:, None, None, None]
        + occ_energy[None, None, None, :]
        - vir_local[None, :, None, None]
        - vir_energy_b[None, None, :, None]
    )
    update = residual / denom
    squares = all_sum(copies)
    total_count = (
        occ_energy.shape[0] * occ_energy.shape[0] * vir_energy_a.shape[0] * vir_energy_b.shape[0]
    )
    residual_rms = jnp.sqrt(squares / total_count)
    return (update, residual_rms)


def solution(mesh):
    return jax.shard_map(
        per_device,
        mesh=mesh,
        in_specs=(
            P("blk", None, "rep", None),
            P("rep", None, "blk", None),
            P("rep", None, "blk", None),
            P(),
            P(),
            P(),
        ),
        out_specs=(P("blk", "rep", None, None), P()),
        check_vma=False,
    )
```
